128 devices in a mesh: rcv: 16 (over y, x), freq: 8 (over z, core).
Axes of the slice: x: 4, y: 4, z: 4, core: 2. Of those that a mesh axis runs over, the one named last changes fastest.
Arguments:
- kernel: bfloat16 [2, 32, 4096, 4096], P(None, 'freq', 'rcv'), may hold values from -0.09375 to 0.09375
- data: float32 [2, 32, 4096, 32], P(None, 'freq', 'rcv'), may hold values from -6 to 6
- cutoffs: int32 [4096], P('rcv'), may hold values from 128 to 1024
Outputs:
- model: float32 [2, 32, 4096, 32], P(None, 'freq', 'rcv')
- residual: float32 [2, 32, 4096, 32], P(None, 'freq', 'rcv')
The draws below stay inside these ranges and needn't reach their ends.
All inputs are finite; a program needn't handle non-finite values.
Results may differ from the reference program's by a relative error of at most 0.018.
Values may be sent and summed in bfloat16 or wider, within the bound.
No kernel may reach another device: no remote copies, remote signals or barrier semaphores. Data moves between devices by JAX's collectives and lax.ppermute only.
A program may use at most 256 MiB of HBM per device.

```python
import math
import jax
import jax.numpy as jnp
from jax import lax

NR = 4096
NV = 4096
C = 32
NT = 1024
ITERS = 2
F = 32
N_RCV = 16


def place_ends(entries, rng, least, top_value):
    longest = entries.shape.index(max(entries.shape))
    spots = []
    for shift in (0, 1):
        where = [jax.random.randint(jax.random.fold_in(rng, axis), (), 0, length) for axis, length in enumerate(entries.shape)]
        where[longest] = (where[longest] + shift) % entries.shape[longest]
        spots.append(tuple(where))
    return entries.at[spots[0]].set(least).at[spots[1]].set(top_value)


def with_spikes(array, key, source, target, parts, factor):
    def block_of(dim):
        return (jnp.arange(array.shape[dim]) // (array.shape[dim] // parts)).reshape((-1,) + (1,) * (array.ndim - 1 - dim))

    one_side = jax.random.permutation(key, parts)[block_of(target)]
    far = (block_of(target) + parts // 2) % parts
    return jnp.where((block_of(source) == one_side) | (block_of(source) == far), factor * array, array)


def shard_levels(stream_key, dims, split, low, high):
    level = 1.0
    for axis_at, shards_of in split:
        heights = jax.random.uniform(jax.random.fold_in(jax.random.fold_in(stream_key, 6), axis_at), (shards_of,), jnp.float32, low / len(split), high / len(split))
        level = level * jnp.repeat(jnp.exp(heights), dims[axis_at] // shards_of).reshape((-1,) + (1,) * (len(dims) - 1 - axis_at))
    return level


def centred(rng, extent, scale, limit, shards=(), held_as=jnp.bfloat16):
    entries = jax.random.normal(rng, extent, jnp.float32) * scale
    if len(shards) > 0:
        entries = shard_levels(rng, extent, shards, -0.22, 0.18) * entries
    return jnp.clip(entries, min=-limit, max=limit).astype(held_as)


def noise_with(key, shape, scale, reach, cuts, heavy, held_as=jnp.bfloat16):
    values = scale * jax.random.normal(key, shape, jnp.float32)
    if cuts:
        values = values * shard_levels(key, shape, cuts, -0.22, 0.18)
    return jnp.clip(with_spikes(values, jax.random.fold_in(key, 3), *heavy), -reach, reach).astype(held_as)


def setup_inputs(seed: int = 0) -> dict:
    streams_of = jax.random.split(jax.random.key(seed), 4)
    return {
        "kernel": noise_with(streams_of[0], (2, F, NR, NV), (2 * NV) ** -0.5, 0.09375, ((1, 8), (2, 16)), (2, 3, 16, 2.0)),
        "data": centred(streams_of[1], (2, F, NR, C), 1.0, 6.0, ((1, 8), (2, 16)), jnp.float32),
        "cutoffs": place_ends(jax.random.randint(streams_of[2], (NV,), NT // 8, NT + 1), jax.random.fold_in(streams_of[2], 1), NT // 8, NT).astype(jnp.int32),
    }


def make_table():
    steps_t = jnp.arange(NT, dtype=jnp.int32)
    bins = jnp.arange(F, dtype=jnp.int32) + 1
    phase = (steps_t[:, None] * bins[None, :] % NT).astype(jnp.float32) * (2.0 * math.pi / NT)
    scale = math.sqrt(2.0 / NT)
    return jnp.concatenate([scale * jnp.cos(phase), -scale * jnp.sin(phase)], axis=1)

def window(values, cutoffs, table):
    width = NV // N_RCV
    count = NV // width
    blocks = jnp.moveaxis(values.reshape(2, F, count, width, C), 2, 0)
    cuts = cutoffs.reshape(count, width)

    def one(pair):
        block, cut = pair
        flat = block.reshape(2 * F, width * C)
        times = jnp.dot(table, flat, precision=lax.Precision.HIGHEST)
        keep = (jnp.arange(NT, dtype=jnp.int32)[:, None] < cut[None, :]).astype(jnp.float32)
        times = (times.reshape(NT, width, C) * keep[:, :, None]).reshape(NT, width * C)
        back = jnp.dot(table.T, times, precision=lax.Precision.HIGHEST)
        return back.reshape(2, F, width, C)
    result = lax.map(one, (blocks, cuts))
    return jnp.moveaxis(result, 0, 2).reshape(2, F, NV, C)

def forward(kernel, shaped):

    def one(pair):
        kern, piece = pair
        joined = jnp.concatenate([piece[0], piece[1]], axis=-1)
        left = jnp.dot(kern[0], joined, preferred_element_type=jnp.float32)
        right = jnp.dot(kern[1], joined, preferred_element_type=jnp.float32)
        return jnp.stack([left[:, :C] - right[:, C:], left[:, C:] + right[:, :C]])
    result = lax.map(one, (jnp.moveaxis(kernel, 1, 0), jnp.moveaxis(shaped, 1, 0)))
    return jnp.moveaxis(result, 0, 1)

def adjoint(kernel, rounded):

    def one(pair):
        kern, piece = pair
        joined = jnp.concatenate([piece[0], piece[1]], axis=-1)
        left = jnp.dot(kern[0].T, joined, preferred_element_type=jnp.float32)
        right = jnp.dot(kern[1].T, joined, preferred_element_type=jnp.float32)
        return jnp.stack([left[:, :C] + right[:, C:], left[:, C:] - right[:, :C]])
    result = lax.map(one, (jnp.moveaxis(kernel, 1, 0), jnp.moveaxis(rounded, 1, 0)))
    return jnp.moveaxis(result, 0, 1)

def reference(kernel, data, cutoffs):
    table = make_table()
    model = jnp.zeros((2, F, NV, C), jnp.float32)
    residual = data
    grad = window(adjoint(kernel, residual.astype(jnp.bfloat16)), cutoffs, table)
    gamma = jnp.sum(grad * grad)
    direction = grad
    for step in range(ITERS):
        shaped = window(direction, cutoffs, table).astype(jnp.bfloat16)
        image = forward(kernel, shaped)
        delta = jnp.sum(image * image)
        alpha = gamma / delta
        model = model + alpha * direction
        residual = residual - alpha * image
        if step + 1 < ITERS:
            grad = window(adjoint(kernel, residual.astype(jnp.bfloat16)), cutoffs, table)
            fresh = jnp.sum(grad * grad)
            direction = grad + fresh / gamma * direction
            gamma = fresh
    return (model, residual)
```

```python
import math

import jax
import jax.numpy as jnp
import numpy as np
from jax import lax
from jax.experimental import pallas as pl
from jax.experimental.pallas import tpu as pltpu
from jax.sharding import PartitionSpec as P

NT = 1024
F = 32
AXES = ("rcv", "freq")
BF = jnp.bfloat16
F32 = jnp.float32
VMEM = pl.BlockSpec(memory_space=pltpu.VMEM)
SMEM = pl.BlockSpec(memory_space=pltpu.SMEM)
NT_DIMS = (((1,), (1,)), ((), ()))


def index(y, x, z, c):
    return (y * 4 + x) * 8 + z * 2 + c


DEVICES = [(y, x, z, c) for y in range(4) for x in range(4) for z in range(4) for c in range(2)]


def move(value, target):
    pairs = [(index(*d), index(*target(*d))) for d in DEVICES]
    return lax.ppermute(value, AXES, pairs)


def along_big(step):
    def target(y, x, z, c):
        return ((y + step) % 4, x, z, c) if c == 0 else (y, (x + step) % 4, z, c)

    return target


def along_small(step):
    def target(y, x, z, c):
        return (y, (x + step) % 4, z, c) if c == 0 else ((y + step) % 4, x, z, c)

    return target


def along_z(step):
    return lambda y, x, z, c: (y, x, (z + step) % 4, c)


def other_core(y, x, z, c):
    return (y, x, z, 1 - c)


def window_matrix():
    bins = np.arange(1, F + 1)
    theta = 2.0 * np.pi / NT

    def ratio(k):
        half = theta * k / 2.0
        safe = np.where(k == 0, 1.0, half)
        return np.where(k == 0, 0.0, 0.5 - 0.5j / np.tan(safe))

    direct = ratio(bins[:, None] - bins[None, :]) / NT
    mirror = ratio(bins[:, None] + bins[None, :]) / NT
    top = np.concatenate([direct.real + mirror.real, -direct.imag + mirror.imag], axis=1)
    low = np.concatenate([direct.imag + mirror.imag, direct.real - mirror.real], axis=1)
    return np.concatenate([top, low], axis=0).astype(np.float32)


def adjoint_kernel(j_ref, u_ref, k_ref, own_ref, oth_ref):
    def group(kb, carry):
        for ks in range(4):
            j = j_ref[kb * 4 + ks]
            cols = pl.ds(pl.multiple_of(j * 256, 256), 256)
            for f in range(4):
                u = u_ref[f]
                v = jnp.concatenate([u[16:32], -u[0:16], u[48:64], -u[32:48]], axis=0)
                r = jnp.dot(u, k_ref[0, f, :, cols], preferred_element_type=F32)
                r = r + jnp.dot(v, k_ref[1, f, :, cols], preferred_element_type=F32)
                r = r.astype(BF)
                own_ref[kb * 4 + ks, f] = r[:32]
                oth_ref[ks * 4 + kb, f] = r[32:]
        return carry

    lax.fori_loop(0, 4, group, 0)


def adjoint(table, u, kernel):
    shape = jax.ShapeDtypeStruct((16, 4, 32, 256), BF)
    return pl.pallas_call(
        adjoint_kernel,
        in_specs=[SMEM, VMEM, VMEM],
        out_specs=[VMEM, VMEM],
        out_shape=[shape, shape],
        compiler_params=pltpu.CompilerParams(vmem_limit_bytes=12 << 20),
        cost_estimate=pl.CostEstimate(flops=2 << 30, bytes_accessed=4 << 20, transcendentals=0),
        name="adjoint",
    )(table, u, kernel)


def forward_kernel(j_ref, own_ref, oth_ref, k_ref, out_ref):
    def one(f, carry):
        acc = jnp.zeros((256, 64), F32)
        for kb in range(4):
            for ks in range(4):
                j = j_ref[kb * 4 + ks]
                cols = pl.ds(pl.multiple_of(j * 256, 256), 256)
                a = own_ref[kb * 4 + ks, f]
                b = oth_ref[ks * 4 + kb, f]
                x = jnp.concatenate([a, b], axis=0)
                t = jnp.concatenate([-a[16:], a[:16], -b[16:], b[:16]], axis=0)
                acc = acc + lax.dot_general(
                    k_ref[0, f, :, cols], x, NT_DIMS, preferred_element_type=F32
                )
                acc = acc + lax.dot_general(
                    k_ref[1, f, :, cols], t, NT_DIMS, preferred_element_type=F32
                )
        out_ref[f] = acc.T
        return carry

    lax.fori_loop(0, 4, one, 0)


def forward(table, own, oth, kernel):
    return pl.pallas_call(
        forward_kernel,
        in_specs=[SMEM, VMEM, VMEM, VMEM],
        out_specs=VMEM,
        out_shape=jax.ShapeDtypeStruct((4, 64, 256), F32),
        compiler_params=pltpu.CompilerParams(vmem_limit_bytes=12 << 20),
        cost_estimate=pl.CostEstimate(flops=2 << 30, bytes_accessed=4 << 20, transcendentals=0),
        name="forward",
    )(table, own, oth, kernel)


def window_kernel(place_ref, a0, a1, a2, a3, m_ref, cos_ref, sin_ref, n_ref, g_ref, s_ref, y, g, s):
    z = place_ref[0]
    core = place_ref[1]
    for k, a in enumerate((a0, a1, a2, a3)):
        base = lax.rem(z + k, 4) * 256
        for half in range(2):
            start = base + (half + core - 2 * half * core) * 128
            rows = pl.ds(pl.multiple_of(start, 128), 128)
            part = a[pl.ds(half * 128, 128), :].astype(F32)
            y[0, rows, :] = part[:, :128]
            y[1, rows, :] = part[:, 128:]

    matrix = m_ref[...]
    cos = cos_ref[...]
    sin = sin_ref[...]
    share = n_ref[...]

    def apply(re, im):
        turned = jnp.concatenate([cos * re - sin * im, sin * re + cos * im], axis=0)
        flat = jnp.concatenate([re, im], axis=0)
        both = jnp.dot(
            matrix,
            jnp.concatenate([flat, turned], axis=1),
            precision=lax.Precision.HIGHEST,
            preferred_element_type=F32,
        )
        plain, w = both[:, :256], both[:, 256:]
        out_re = share * re + plain[:F] - cos * w[:F] - sin * w[F:]
        out_im = share * im + plain[F:] - cos * w[F:] + sin * w[:F]
        return out_re, out_im

    def take(ref, first):
        rows = pl.ds(first, F, stride=32)
        return jnp.concatenate([ref[0, rows, :], ref[1, rows, :]], axis=1)

    def put(ref, first, value):
        rows = pl.ds(first, F, stride=32)
        ref[0, rows, :] = value[:, :128]
        ref[1, rows, :] = value[:, 128:]

    def one(c, carry):
        re, im = apply(take(y, c), take(y, c + 16))
        put(g, c, re)
        put(g, c + 16, im)
        re, im = apply(re, im)
        put(s, c, re)
        put(s, c + 16, im)
        return carry

    lax.fori_loop(0, 16, one, 0)
    for half in range(2):
        start = z * 256 + (half + core - 2 * half * core) * 128
        rows = pl.ds(pl.multiple_of(start, 128), 128)
        g_ref[half] = jnp.concatenate([g[0, rows, :], g[1, rows, :]], axis=1)
        s_ref[half] = jnp.concatenate([s[0, rows, :], s[1, rows, :]], axis=1).astype(BF)


def window(place, blocks, matrix, cos, sin, share):
    return pl.pallas_call(
        window_kernel,
        in_specs=[SMEM] + [VMEM] * 8,
        out_specs=[VMEM, VMEM],
        out_shape=[
            jax.ShapeDtypeStruct((2, 128, 256), F32),
            jax.ShapeDtypeStruct((2, 128, 256), BF),
        ],
        scratch_shapes=[pltpu.VMEM((2, 1024, 128), F32)] * 3,
        compiler_params=pltpu.CompilerParams(vmem_limit_bytes=12 << 20),
        cost_estimate=pl.CostEstimate(flops=1 << 29, bytes_accessed=2 << 20, transcendentals=0),
        name="window",
    )(place, *blocks, matrix, cos, sin, share)


def total(values):
    values = values + move(values, other_core)
    for axis in (along_z, along_small, along_big):
        values = values + move(values, axis(1)) + move(values, axis(2)) + move(values, axis(3))
    return values


def body(kernel, data, cutoffs):
    rcv = lax.axis_index("rcv")
    freq = lax.axis_index("freq")
    yy, xx, zz, core = rcv // 4, rcv % 4, freq // 2, freq % 2
    place = jnp.stack([zz, core]).astype(jnp.int32)
    far = jnp.arange(16, dtype=jnp.int32) // 4
    near = jnp.arange(16, dtype=jnp.int32) % 4
    off_y = jnp.where(core == 0, far, near)
    off_x = jnp.where(core == 0, near, far)
    table = (yy + off_y) % 4 * 4 + (xx + off_x) % 4

    kernel = pltpu.with_memory_space_constraint(kernel, pltpu.VMEM)
    matrix = jnp.asarray(window_matrix())
    bins = jnp.arange(1, F + 1, dtype=jnp.int32)
    phase = (bins[:, None] * cutoffs[None, :] % NT).astype(F32) * (2.0 * math.pi / NT)
    cos, sin = jnp.cos(phase), jnp.sin(phase)
    share = (cutoffs.astype(F32) / NT)[None, :]

    def by_half(t):
        t = t.reshape(2, 4, 2, 16, 256).transpose(1, 2, 0, 3, 4)
        return jnp.where(core == 0, t, t[:, ::-1]).reshape(4, 64, 256)

    def from_half(t):
        t = t.reshape(4, 2, 2, 16, 256)
        t = jnp.where(core == 0, t, t[:, ::-1])
        return t.transpose(2, 0, 1, 3, 4).reshape(2, 4, 32, 256)

    def gather_terms(u):
        own, oth = adjoint(table, u, kernel)
        got = move(oth, other_core)
        own = own.reshape(4, 4, 128, 256)
        got = got.reshape(4, 4, 128, 256)
        pair = [jnp.stack([own[kb], got[kb]], axis=1) for kb in range(4)]
        rest = pair[0][1:].astype(F32)
        mine = pair[0][0].astype(F32)
        for kb in (2, 1, 3):
            rest = rest + move(pair[kb][1:], along_big(kb)).astype(F32)
        for kb in (2, 1, 3):
            mine = mine + move(pair[kb][0], along_big(kb)).astype(F32)
        rest = rest.astype(BF)
        for ks in (2, 1, 3):
            mine = mine + move(rest[ks - 1], along_small(ks)).astype(F32)
        mine = mine.astype(BF).reshape(256, 256)
        return [mine] + [move(mine, along_z(-k)) for k in (1, 2, 3)]

    def image_of(shaped):
        near = [shaped] + [move(shaped, along_small(-ks)) for ks in (1, 2, 3)]
        rest = jnp.stack(near[1:])
        blocks = [jnp.stack(near)]
        for kb in (1, 2, 3):
            first = move(shaped, along_big(-kb))
            more = move(rest, along_big(-kb))
            blocks.append(jnp.concatenate([first[None], more], axis=0))
        blocks = jnp.concatenate(blocks, axis=0)
        own = blocks[:, 0]
        oth = move(blocks[:, 1], other_core)
        return forward(
            table, own.reshape(16, 4, 32, 256), oth.reshape(16, 4, 32, 256), kernel
        )

    def windowed(blocks):
        return window(place, blocks, matrix, cos, sin, share)

    start = jnp.swapaxes(data, 2, 3)
    g0, s0 = windowed(gather_terms(by_half(start.astype(BF))))
    i0 = image_of(s0)
    h, s1 = windowed(gather_terms(i0.astype(BF)))
    i1 = image_of(s1)

    sums = [
        jnp.sum(g0 * g0),
        jnp.sum(g0 * h),
        jnp.sum(h * h),
        jnp.sum(i0 * i0),
        jnp.sum(i0 * i1),
        jnp.sum(i1 * i1),
    ]
    sums = total(jnp.stack(sums + [jnp.zeros((), F32)] * 2))
    gg, gh, hh, ii, ij, jj = [sums[k] for k in range(6)]
    alpha0 = gg / ii
    fresh = gg - 2.0 * alpha0 * gh + alpha0 * alpha0 * hh
    stay = 1.0 + fresh / gg
    delta = stay * stay * ii - 2.0 * stay * alpha0 * ij + alpha0 * alpha0 * jj
    alpha1 = fresh / delta
    on_first = alpha0 + alpha1 * stay
    on_second = alpha1 * alpha0

    def whole(t):
        got = move(t[1].astype(BF), other_core).astype(F32)
        joined = jnp.stack([t[0].reshape(4, 32, 256), got.reshape(4, 32, 256)], axis=1)
        return joined.reshape(4, 64, 256)

    model = from_half(on_first * whole(g0) - on_second * whole(h))
    residual = start - from_half(on_first * i0 - on_second * i1)
    return jnp.swapaxes(model, 2, 3), jnp.swapaxes(residual, 2, 3)


def solution(mesh):
    placed = P(None, "freq", "rcv", None)
    return jax.shard_map(
        body,
        mesh=mesh,
        in_specs=(placed, placed, P("rcv")),
        out_specs=(placed, placed),
        check_vma=False,
    )
```

```python
import math

import jax
import jax.numpy as jnp
import numpy as np
from jax import lax
from jax.experimental import pallas as pl
from jax.experimental.pallas import tpu as pltpu
from jax.sharding import PartitionSpec as P

NT = 1024
F = 32
AXES = ("rcv", "freq")
BF = jnp.bfloat16
F32 = jnp.float32
VMEM = pl.BlockSpec(memory_space=pltpu.VMEM)
HBM = pl.BlockSpec(memory_space=pltpu.HBM)
CC = 16
SMEM = pl.BlockSpec(memory_space=pltpu.SMEM)
NT_DIMS = (((1,), (1,)), ((), ()))


def index(y, x, z, c):
    return (y * 4 + x) * 8 + z * 2 + c


DEVICES = [(y, x, z, c) for y in range(4) for x in range(4) for z in range(4) for c in range(2)]


def move(value, target):
    pairs = [(index(*d), index(*target(*d))) for d in DEVICES]
    return lax.ppermute(value, AXES, pairs)


def along_big(step):
    def target(y, x, z, c):
        return ((y + step) % 4, x, z, c) if c == 0 else (y, (x + step) % 4, z, c)

    return target


def along_small(step):
    def target(y, x, z, c):
        return (y, (x + step) % 4, z, c) if c == 0 else ((y + step) % 4, x, z, c)

    return target


def along_z(step):
    return lambda y, x, z, c: (y, x, (z + step) % 4, c)


def other_core(y, x, z, c):
    return (y, x, z, 1 - c)


def window_matrix():
    bins = np.arange(1, F + 1)
    theta = 2.0 * np.pi / NT

    def ratio(k):
        half = theta * k / 2.0
        safe = np.where(k == 0, 1.0, half)
        return np.where(k == 0, 0.0, 0.5 - 0.5j / np.tan(safe))

    direct = ratio(bins[:, None] - bins[None, :]) / NT
    mirror = ratio(bins[:, None] + bins[None, :]) / NT
    top = np.concatenate([direct.real + mirror.real, -direct.imag + mirror.imag], axis=1)
    low = np.concatenate([direct.imag + mirror.imag, direct.real - mirror.real], axis=1)
    return np.concatenate([top, low], axis=0).astype(np.float32)


def cost(flops):
    return pl.CostEstimate(flops=flops, bytes_accessed=4 << 20, transcendentals=0)


def params(mib):
    return pltpu.CompilerParams(vmem_limit_bytes=mib << 20)


def swapped(v, sign):
    rows = []
    for k in range(0, 64, 32):
        rows += [sign * v[k + 16 : k + 32], -sign * v[k : k + 16]]
    return jnp.concatenate(rows, axis=0)


def terms(kb, f, u, j_ref, k_ref, out_ref):
    v = swapped(u, 1)
    for ks in range(4):
        cols = pl.ds(pl.multiple_of(j_ref[kb * 4 + ks] * 256, 256), 256)
        r = jnp.dot(u, k_ref[0, f, :, cols], preferred_element_type=F32)
        r = r + jnp.dot(v, k_ref[1, f, :, cols], preferred_element_type=F32)
        out_ref[ks, f] = r.astype(BF)


def first_kernel(place_ref, j_ref, data_hbm, k_hbm, k_ref, *refs):
    out_refs, (data_ref, sem, sems) = refs[:4], refs[4:]
    core = place_ref[1]
    fetch = pltpu.make_async_copy(data_hbm, data_ref, sem)
    fetch.start()
    copies = [
        [pltpu.make_async_copy(k_hbm.at[p, f], k_ref.at[p, f], sems.at[p, f]) for p in range(2)]
        for f in range(4)
    ]
    for f in range(2):
        for p in range(2):
            copies[f][p].start()
    fetch.wait()
    for f in range(4):
        rows = []
        for half in range(2):
            at = pl.ds(pl.multiple_of((half + core - 2 * half * core) * 16, 16), 16)
            rows += [data_ref[0, f, at, :], data_ref[1, f, at, :]]
        u = jnp.concatenate(rows, axis=0).astype(BF)
        for p in range(2):
            copies[f][p].wait()
            if f < 2:
                copies[f + 2][p].start()
        for kb in range(4):
            terms(kb, f, u, j_ref, k_ref, out_refs[kb])


TERMS = jax.ShapeDtypeStruct((4, 4, 64, 256), BF)


def first_adjoint(place, table, data, kernel):
    return pl.pallas_call(
        first_kernel,
        in_specs=[SMEM, SMEM, HBM, HBM],
        out_specs=[VMEM] * 5,
        out_shape=[pltpu.VMEM(kernel.shape, BF)] + [TERMS] * 4,
        scratch_shapes=[
            pltpu.VMEM(data.shape, F32),
            pltpu.SemaphoreType.DMA,
            pltpu.SemaphoreType.DMA((2, 4)),
        ],
        compiler_params=params(8),
        cost_estimate=cost(4 << 30),
        name="first_adjoint",
    )(
        place,
        table,
        pltpu.with_memory_space_constraint(data, pltpu.HBM),
        pltpu.with_memory_space_constraint(kernel, pltpu.HBM),
    )


def adjoint_kernel(kbs, j_ref, u_ref, k_ref, *out_refs):
    for f in range(4):
        u = u_ref[f].astype(BF)
        for kb, out_ref in zip(kbs, out_refs):
            terms(kb, f, u, j_ref, k_ref, out_ref)


def adjoint(table, u, kernel, kbs):
    return pl.pallas_call(
        lambda *refs: adjoint_kernel(kbs, *refs),
        in_specs=[SMEM, VMEM, VMEM],
        out_specs=[VMEM] * len(kbs),
        out_shape=[TERMS] * len(kbs),
        compiler_params=params(8),
        cost_estimate=cost(len(kbs) << 33),
        name="adjoint",
    )(table, u, kernel)


def fold(v):
    v = jnp.sum(v, axis=0, keepdims=True)
    return v[:, :128] + v[:, 128:]


def forward_kernel(kb, last, second, j_ref, x_ref, k_ref, *refs):
    if kb > 0:
        before_ref, *refs = refs
    if second:
        i0_ref, gg_ref, hh_ref, ii_ref, *refs = refs
    out_ref = refs[0]

    zero = jnp.zeros((1, 128), F32)
    sums = [zero, zero]
    for f in range(4):
        acc = jnp.zeros((256, 64), F32)
        for ks in range(4):
            cols = pl.ds(pl.multiple_of(j_ref[kb * 4 + ks] * 256, 256), 256)
            x = x_ref[ks, f]
            acc = acc + lax.dot_general(
                k_ref[0, f, :, cols], x, NT_DIMS, preferred_element_type=F32
            )
            acc = acc + lax.dot_general(
                k_ref[1, f, :, cols], swapped(x, -1), NT_DIMS, preferred_element_type=F32
            )
        out = acc.T
        if kb > 0:
            out = out + before_ref[f]
        out_ref[f] = out
        if second:
            sums[0] = sums[0] + fold(i0_ref[f] * out)
        if last:
            sums[1] = sums[1] + fold(out * out)
    if second:
        rows = [gg_ref[0:1], hh_ref[0:2], ii_ref[0:1], *sums, zero, zero]
        refs[1][...] = jnp.concatenate(rows, axis=0)
    elif last:
        refs[1][...] = jnp.broadcast_to(sums[1], (8, 128))


def forward(kb, table, blocks, kernel, before=None, last=False, more=()):
    inputs = (blocks, kernel) + (() if before is None else (before,)) + tuple(more)
    out = [jax.ShapeDtypeStruct((4, 64, 256), F32)]
    if last:
        out.append(jax.ShapeDtypeStruct((8, 128), F32))
    return pl.pallas_call(
        lambda *refs: forward_kernel(kb, last, len(more) > 0, *refs),
        in_specs=[SMEM] + [VMEM] * len(inputs),
        out_specs=[VMEM] * len(out),
        out_shape=out,
        compiler_params=params(8),
        cost_estimate=cost(1 << 33),
        name="forward",
    )(table, *inputs)


def parts_of(x):
    high = x.astype(BF)
    low = (x - high.astype(F32)).astype(BF)
    return jnp.concatenate([high, high, low], axis=0)


def window_kernel(second, place_ref, a0, a1, a2, a3, m_ref, mo_ref, cos_ref, sin_ref, n_ref, *refs):
    if second:
        g0_ref, g_ref, s_ref, sum_ref, y, g, s = refs
    else:
        g_ref, s_ref, sum_ref, y, g, s = refs
    z = place_ref[0]
    core = place_ref[1]

    size = 8 * CC

    def swap(half):
        return half + core - 2 * half * core

    for k, a in enumerate((a0, a1, a2, a3)):
        for half in range(2):
            at = (lax.rem(z + k, 4) * 2 + swap(half)) * size
            rows = pl.ds(pl.multiple_of(at, size), size)
            part = a[pl.ds(half * size, size), :].astype(F32)
            y[0, rows, :] = part[:, :128]
            y[1, rows, :] = part[:, 128:]

    cos = cos_ref[...]
    sin = sin_ref[...]
    share = n_ref[...]
    eight = pl.ds(pl.multiple_of(z * 8, 8), 8)
    cos_own = cos_ref[eight, :]
    sin_own = sin_ref[eight, :]

    def take(ref, first, count):
        rows = pl.ds(first, count, stride=2 * CC)
        return jnp.concatenate([ref[0, rows, :], ref[1, rows, :]], axis=1)

    def put(ref, first, value):
        rows = pl.ds(first, value.shape[0], stride=2 * CC)
        ref[0, rows, :] = value[:, :128]
        ref[1, rows, :] = value[:, 128:]

    def products(matrix, pairs):
        columns = []
        for re, im in pairs:
            columns.append(parts_of(jnp.concatenate([re, im], axis=0)))
            turned = jnp.concatenate([cos * re - sin * im, sin * re + cos * im], axis=0)
            columns.append(parts_of(turned))
        return jnp.dot(matrix, jnp.concatenate(columns, axis=1), preferred_element_type=F32)

    def combine(re, im, both, at, c, d):
        n = re.shape[0]
        plain = both[:, at * 512 : at * 512 + 256]
        w = both[:, at * 512 + 256 : at * 512 + 512]
        out_re = share * re + plain[:n] - c * w[:n] - d * w[n:]
        out_im = share * im + plain[n:] - c * w[n:] + d * w[:n]
        return out_re, out_im

    def four(step, carry):
        first = step * 4
        pairs = [(take(y, first + i, F), take(y, first + i + CC, F)) for i in range(4)]
        both = products(m_ref[...], pairs)
        grads = []
        for i, (re, im) in enumerate(pairs):
            re, im = combine(re, im, both, i, cos, sin)
            put(g, first + i, re)
            put(g, first + i + CC, im)
            grads.append((re, im))
        both = products(mo_ref[z], grads)
        for i in range(4):
            re = take(g, z * 2 * size + first + i, 8)
            im = take(g, z * 2 * size + first + i + CC, 8)
            re, im = combine(re, im, both, i, cos_own, sin_own)
            put(s, first + i, re)
            put(s, first + i + CC, im)
        return carry

    lax.fori_loop(0, CC // 4, four, 0)
    sums = [jnp.zeros((1, 128), F32)] * 2
    for half in range(2):
        rows = pl.ds(pl.multiple_of((z * 2 + swap(half)) * size, size), size)
        value = jnp.concatenate([g[0, rows, :], g[1, rows, :]], axis=1)
        g_ref[half] = value
        if second:
            sums = [sums[0] + fold(g0_ref[half] * value), sums[1] + fold(value * value)]
        else:
            sums = [sums[0] + fold(value * value), sums[1]]
        rows = pl.ds(pl.multiple_of(swap(half) * size, size), size)
        s_ref[half] = jnp.concatenate([s[0, rows, :], s[1, rows, :]], axis=1).astype(BF)
    sum_ref[...] = jnp.concatenate(sums + [jnp.zeros((6, 128), F32)], axis=0)


def window(place, blocks, constants, *more):
    return pl.pallas_call(
        lambda *refs: window_kernel(len(more) > 0, *refs),
        in_specs=[SMEM] + [VMEM] * (9 + len(more)),
        out_specs=[VMEM, VMEM, VMEM],
        out_shape=[
            jax.ShapeDtypeStruct((2, 8 * CC, 256), F32),
            jax.ShapeDtypeStruct((2, 8 * CC, 256), BF),
            jax.ShapeDtypeStruct((8, 128), F32),
        ],
        scratch_shapes=[pltpu.VMEM((2, 64 * CC, 128), F32)] * 2
        + [pltpu.VMEM((2, 16 * CC, 128), F32)],
        compiler_params=params(12),
        cost_estimate=cost(1 << 30),
        name="window",
    )(place, *blocks, *constants, *more)


def last_kernel(place_ref, sum_ref, i0, i1, data_ref, g0, g0_got, h, h_got, model_ref, res_ref):
    core = place_ref[1]
    sums = jnp.sum(sum_ref[...], axis=1, keepdims=True)
    gg, gh, hh, ii, ij, jj = [sums[k : k + 1] for k in range(6)]
    alpha0 = gg / ii
    fresh = gg - 2.0 * alpha0 * gh + alpha0 * alpha0 * hh
    stay = 1.0 + fresh / gg
    delta = stay * stay * ii - 2.0 * stay * alpha0 * ij + alpha0 * alpha0 * jj
    alpha1 = fresh / delta
    on_first = alpha0 + alpha1 * stay
    on_second = alpha1 * alpha0
    for half in range(2):
        at = pl.ds(pl.multiple_of((half + core - 2 * half * core) * 16, 16), 16)
        for f in range(4):
            for p in range(2):
                rows = slice(f * 32 + p * 16, f * 32 + p * 16 + 16)
                left = g0[0, rows, :] if half == 0 else g0_got[rows, :]
                right = h[0, rows, :] if half == 0 else h_got[rows, :]
                model_ref[p, f, at, :] = on_first * left - on_second * right
                rows = slice(half * 32 + p * 16, half * 32 + p * 16 + 16)
                change = on_first * i0[f, rows, :] - on_second * i1[f, rows, :]
                res_ref[p, f, at, :] = data_ref[p, f, at, :] - change


def last(place, *arrays):
    shape = jax.ShapeDtypeStruct((2, 4, 32, 256), F32)
    return pl.pallas_call(
        last_kernel,
        in_specs=[SMEM] + [VMEM] * len(arrays),
        out_specs=[VMEM, VMEM],
        out_shape=[shape, shape],
        compiler_params=params(8),
        cost_estimate=cost(1 << 20),
        name="last",
    )(place, *arrays)


def total(values):
    values = values + move(values, other_core)
    for axis in (along_z, along_small, along_big):
        values = values + move(values, axis(1)) + move(values, axis(2)) + move(values, axis(3))
    return values


def body(kernel, data, cutoffs):
    rcv = lax.axis_index("rcv")
    freq = lax.axis_index("freq")
    yy, xx, zz, core = rcv // 4, rcv % 4, freq // 2, freq % 2
    place = jnp.stack([zz, core]).astype(jnp.int32)
    far = jnp.arange(16, dtype=jnp.int32) // 4
    near = jnp.arange(16, dtype=jnp.int32) % 4
    off_y = jnp.where(core == 0, far, near)
    off_x = jnp.where(core == 0, near, far)
    table = (yy + off_y) % 4 * 4 + (xx + off_x) % 4

    matrix = window_matrix()
    high = matrix.astype(jnp.bfloat16)
    low = (matrix - high.astype(np.float32)).astype(jnp.bfloat16)
    stacked = jnp.asarray(np.concatenate([high, low, high], axis=1))
    own_rows = stacked.reshape(2, 4, 8, 192).swapaxes(0, 1).reshape(4, 16, 192)
    bins = jnp.arange(1, F + 1, dtype=jnp.int32)
    phase = (bins[:, None] * cutoffs[None, :] % NT).astype(F32) * (2.0 * math.pi / NT)
    share = (cutoffs.astype(F32) / NT)[None, :]
    constants = (stacked, own_rows, jnp.cos(phase), jnp.sin(phase), share)

    def summed(parts):
        out = parts[0].astype(F32)
        for part in parts[1:]:
            out = out + part.astype(F32)
        return out.astype(BF)

    def gather_terms(own):
        got = [move(own[kb], along_big(kb)) for kb in (2, 1, 3)]
        row = [summed([own[0][ks]] + [part[ks] for part in got]) for ks in range(4)]
        mine = summed([row[0]] + [move(row[ks], along_small(ks)) for ks in (2, 1, 3)])
        mine = mine.reshape(4, 2, 32, 256)
        mine = jnp.stack([mine[:, 0], move(mine[:, 1], other_core)]).reshape(256, 256)
        return [mine] + [move(mine, along_z(-k)) for k in (1, 2, 3)]

    def image_of(shaped, *more):
        shaped = shaped.reshape(2, 4, 32, 256)
        shaped = jnp.stack([shaped[0], move(shaped[1], other_core)], axis=1).reshape(4, 64, 256)
        row = jnp.stack([shaped] + [move(shaped, along_small(-ks)) for ks in (1, 2, 3)])
        near = {kb: move(row, along_big(-kb)) for kb in (1, 3)}
        (out,) = forward(0, table, row, held)
        row, out = lax.optimization_barrier((row, out))
        far = move(row, along_big(-2))
        for kb in (1, 3):
            (out,) = forward(kb, table, near[kb], held, out)
        return forward(2, table, far, held, out, True, more)

    start = jnp.swapaxes(data, 2, 3)
    held, *own = first_adjoint(place, table, start, kernel)
    held = pltpu.with_memory_space_constraint(held, pltpu.VMEM)
    g0, s0, gg = window(place, gather_terms(own), constants)
    i0, ii = image_of(s0)
    far = adjoint(table, i0, held, (2,))
    rest = adjoint(table, i0, held, (0, 1, 3))
    h, s1, hh = window(place, gather_terms([*rest[:2], far[0], rest[2]]), constants, g0)
    i1, sums = image_of(s1, i0, gg, hh, ii)
    g0_got = move(g0[1], other_core)
    h_got = move(h[1], other_core)
    model, residual = last(place, total(sums), i0, i1, start, g0, g0_got, h, h_got)
    return jnp.swapaxes(model, 2, 3), jnp.swapaxes(residual, 2, 3)


def solution(mesh):
    placed = P(None, "freq", "rcv", None)
    return jax.shard_map(
        body,
        mesh=mesh,
        in_specs=(placed, placed, P("rcv")),
        out_specs=(placed, placed),
        check_vma=False,
    )
```

```python
import math

import jax
import jax.numpy as jnp
import numpy as np
from jax import lax
from jax.experimental import pallas as pl
from jax.experimental.pallas import tpu as pltpu
from jax.sharding import PartitionSpec as P

NT = 1024
F = 32
AXES = ("rcv", "freq")
BF = jnp.bfloat16
F32 = jnp.float32
VMEM = pl.BlockSpec(memory_space=pltpu.VMEM)
HBM = pl.BlockSpec(memory_space=pltpu.HBM)
CC = 16
SMEM = pl.BlockSpec(memory_space=pltpu.SMEM)
NT_DIMS = (((1,), (1,)), ((), ()))


def index(y, x, z, c):
    return (y * 4 + x) * 8 + z * 2 + c


DEVICES = [(y, x, z, c) for y in range(4) for x in range(4) for z in range(4) for c in range(2)]


def move(value, target):
    pairs = [(index(*d), index(*target(*d))) for d in DEVICES]
    return lax.ppermute(value, AXES, pairs)


def along_big(step):
    def target(y, x, z, c):
        return ((y + step) % 4, x, z, c) if c == 0 else (y, (x + step) % 4, z, c)

    return target


def along_small(step):
    def target(y, x, z, c):
        return (y, (x + step) % 4, z, c) if c == 0 else ((y + step) % 4, x, z, c)

    return target


def along_z(step):
    return lambda y, x, z, c: (y, x, (z + step) % 4, c)


def other_core(y, x, z, c):
    return (y, x, z, 1 - c)


def window_matrix():
    bins = np.arange(1, F + 1)
    theta = 2.0 * np.pi / NT

    def ratio(k):
        half = theta * k / 2.0
        safe = np.where(k == 0, 1.0, half)
        return np.where(k == 0, 0.0, 0.5 - 0.5j / np.tan(safe))

    direct = ratio(bins[:, None] - bins[None, :]) / NT
    mirror = ratio(bins[:, None] + bins[None, :]) / NT
    top = np.concatenate([direct.real + mirror.real, -direct.imag + mirror.imag], axis=1)
    low = np.concatenate([direct.imag + mirror.imag, direct.real - mirror.real], axis=1)
    return np.concatenate([top, low], axis=0).astype(np.float32)


def cost(flops):
    return pl.CostEstimate(flops=flops, bytes_accessed=4 << 20, transcendentals=0)


def params(mib):
    return pltpu.CompilerParams(vmem_limit_bytes=mib << 20)


def swapped(v, sign):
    rows = []
    for k in range(0, 64, 32):
        rows += [sign * v[k + 16 : k + 32], -sign * v[k : k + 16]]
    return jnp.concatenate(rows, axis=0)


def terms(kb, f, u, at, j_ref, k_ref, out_ref):
    v = swapped(u, 1)
    for ks in range(4):
        cols = pl.ds(pl.multiple_of(j_ref[kb * 4 + ks] * 256, 256), 256)
        r = jnp.dot(u, k_ref[0, f, :, cols], preferred_element_type=F32)
        r = r + jnp.dot(v, k_ref[1, f, :, cols], preferred_element_type=F32)
        out_ref[ks, at] = r.astype(BF)


def first_kernel(place_ref, j_ref, data_hbm, k_hbm, *refs):
    held_refs, turned_refs, out_refs = refs[:2], refs[2:4], refs[4:8]
    data_ref, sem, sems = refs[8:]
    core = place_ref[1]
    fetch = pltpu.make_async_copy(data_hbm, data_ref, sem)
    fetch.start()
    copies = [
        [
            pltpu.make_async_copy(k_hbm.at[p, f], held_refs[f // 2].at[p, f % 2], sems.at[p, f])
            for p in range(2)
        ]
        for f in range(4)
    ]
    for f in range(2):
        for p in range(2):
            copies[f][p].start()
    fetch.wait()
    for f in range(4):
        rows = []
        for half in range(2):
            at = pl.ds(pl.multiple_of((half + core - 2 * half * core) * 16, 16), 16)
            rows += [data_ref[0, f, at, :], data_ref[1, f, at, :]]
        u = jnp.concatenate(rows, axis=0).astype(BF)
        for p in range(2):
            copies[f][p].wait()
            if f < 2:
                copies[f + 2][p].start()
        for kb in range(4):
            k_ref = held_refs[f // 2]
            terms(kb, f % 2, u, f, j_ref, k_ref, out_refs[kb])
            for p in range(2):
                for j in range(kb * 4, kb * 4 + 4):
                    at = slice(j * 256, j * 256 + 256)
                    turned_refs[f // 2][p, f % 2, at, :] = k_ref[p, f % 2, :, at].T


def first_adjoint(place, table, data, kernel):
    return pl.pallas_call(
        first_kernel,
        in_specs=[SMEM, SMEM, HBM, HBM],
        out_specs=[VMEM] * 8,
        out_shape=[pltpu.VMEM((2, 2, 256, 4096), BF)] * 2
        + [pltpu.VMEM((2, 2, 4096, 256), BF)] * 2
        + [jax.ShapeDtypeStruct((4, 4, 64, 256), BF)] * 4,
        scratch_shapes=[
            pltpu.VMEM(data.shape, F32),
            pltpu.SemaphoreType.DMA,
            pltpu.SemaphoreType.DMA((2, 4)),
        ],
        compiler_params=params(8),
        cost_estimate=cost(1 << 33),
        name="first_adjoint",
    )(
        place,
        table,
        pltpu.with_memory_space_constraint(data, pltpu.HBM),
        pltpu.with_memory_space_constraint(kernel, pltpu.HBM),
    )


TERMS = jax.ShapeDtypeStruct((4, 2, 64, 256), BF)


def adjoint_kernel(j_ref, u_ref, k_ref, *out_refs):
    for f in range(2):
        u = u_ref[f].astype(BF)
        for kb in (2, 1, 3, 0):
            terms(kb, f, u, f, j_ref, k_ref, out_refs[kb])


def adjoint(table, u, kernel):
    return pl.pallas_call(
        adjoint_kernel,
        in_specs=[SMEM, VMEM, VMEM],
        out_specs=[VMEM] * 4,
        out_shape=[TERMS] * 4,
        compiler_params=params(8),
        cost_estimate=cost(1 << 31),
        name="adjoint",
    )(table, u, kernel)


def fold(v):
    v = jnp.sum(v, axis=0, keepdims=True)
    return v[:, :128] + v[:, 128:]


def forward_kernel(kbs, first, last, second, early, j_ref, k_ref, *refs):
    x_refs, refs = refs[: len(kbs)], refs[len(kbs) :]
    if not first:
        before_ref, *refs = refs
    if second:
        i0_ref, *refs = refs
    early_refs, refs = refs[:early], refs[early:]
    out_ref = refs[0]

    zero = jnp.zeros((1, 128), F32)
    sums = [zero, zero]
    for f in range(2):
        out = jnp.zeros((64, 256), F32) if first else before_ref[f]
        for kb, x_ref in zip(kbs, x_refs):
            for ks in range(4):
                rows = pl.ds(pl.multiple_of(j_ref[kb * 4 + ks] * 256, 256), 256)
                x = x_ref[ks, f]
                out = out + jnp.dot(x, k_ref[0, f, rows, :], preferred_element_type=F32)
                out = out + jnp.dot(
                    swapped(x, -1), k_ref[1, f, rows, :], preferred_element_type=F32
                )
        out_ref[f] = out
        if second:
            sums[0] = sums[0] + fold(i0_ref[f] * out)
        if last:
            sums[1] = sums[1] + fold(out * out)
    if early:
        gg, hh, ii0, ii1, other = [ref[...] for ref in early_refs]
        rows = [gg[0:1], hh[0:2], ii0[1:2] + ii1[1:2]]
        rows += [other[0:1] + sums[0], other[1:2] + sums[1], zero, zero]
        refs[1][...] = jnp.concatenate(rows, axis=0)
    elif last:
        refs[1][...] = jnp.concatenate(sums + [jnp.zeros((6, 128), F32)], axis=0)


def forward(kbs, table, kernel, blocks, before=None, last=False, i0=None, early=()):
    inputs = [kernel, *blocks]
    inputs += [a for a in (before, i0) if a is not None] + list(early)
    out = [jax.ShapeDtypeStruct((2, 64, 256), F32)]
    if last:
        out.append(jax.ShapeDtypeStruct((8, 128), F32))
    flags = (kbs, before is None, last, i0 is not None, len(early))
    return pl.pallas_call(
        lambda *refs: forward_kernel(*flags, *refs),
        in_specs=[SMEM] + [VMEM] * len(inputs),
        out_specs=[VMEM] * len(out),
        out_shape=out,
        compiler_params=params(8),
        cost_estimate=cost(1 << 31),
        name="forward",
    )(table, *inputs)


def parts_of(x):
    high = x.astype(BF)
    low = (x - high.astype(F32)).astype(BF)
    return jnp.concatenate([high, high, low], axis=0)


def window_kernel(second, place_ref, a0, a1, a2, a3, m_ref, mo_ref, cos_ref, sin_ref, n_ref, *refs):
    if second:
        g0_ref, g_ref, s_ref, sum_ref, y, g, s = refs
    else:
        g_ref, s_ref, sum_ref, y, g, s = refs
    z = place_ref[0]
    core = place_ref[1]

    size = 8 * CC

    def swap(half):
        return half + core - 2 * half * core

    for k, a in enumerate((a0, a1, a2, a3)):
        for half in range(2):
            at = (lax.rem(z + k, 4) * 2 + swap(half)) * size
            rows = pl.ds(pl.multiple_of(at, size), size)
            part = a[pl.ds(half * size, size), :].astype(F32)
            y[0, rows, :] = part[:, :128]
            y[1, rows, :] = part[:, 128:]

    cos = cos_ref[...]
    sin = sin_ref[...]
    share = n_ref[...]
    eight = pl.ds(pl.multiple_of(z * 8, 8), 8)
    cos_own = cos_ref[eight, :]
    sin_own = sin_ref[eight, :]

    def take(ref, first, count):
        rows = pl.ds(first, count, stride=2 * CC)
        return jnp.concatenate([ref[0, rows, :], ref[1, rows, :]], axis=1)

    def put(ref, first, value):
        rows = pl.ds(first, value.shape[0], stride=2 * CC)
        ref[0, rows, :] = value[:, :128]
        ref[1, rows, :] = value[:, 128:]

    def products(matrix, pairs):
        columns = []
        for re, im in pairs:
            columns.append(parts_of(jnp.concatenate([re, im], axis=0)))
            turned = jnp.concatenate([cos * re - sin * im, sin * re + cos * im], axis=0)
            columns.append(parts_of(turned))
        return jnp.dot(matrix, jnp.concatenate(columns, axis=1), preferred_element_type=F32)

    def combine(re, im, both, at, c, d):
        n = re.shape[0]
        plain = both[:, at * 512 : at * 512 + 256]
        w = both[:, at * 512 + 256 : at * 512 + 512]
        out_re = share * re + plain[:n] - c * w[:n] - d * w[n:]
        out_im = share * im + plain[n:] - c * w[n:] + d * w[:n]
        return out_re, out_im

    def four(step, carry):
        first = step * 4
        pairs = [(take(y, first + i, F), take(y, first + i + CC, F)) for i in range(4)]
        both = products(m_ref[...], pairs)
        grads = []
        for i, (re, im) in enumerate(pairs):
            re, im = combine(re, im, both, i, cos, sin)
            put(g, first + i, re)
            put(g, first + i + CC, im)
            grads.append((re, im))
        both = products(mo_ref[z], grads)
        for i in range(4):
            re = take(g, z * 2 * size + first + i, 8)
            im = take(g, z * 2 * size + first + i + CC, 8)
            re, im = combine(re, im, both, i, cos_own, sin_own)
            put(s, first + i, re)
            put(s, first + i + CC, im)
        return carry

    lax.fori_loop(0, CC // 4, four, 0)
    sums = [jnp.zeros((1, 128), F32)] * 2
    for half in range(2):
        rows = pl.ds(pl.multiple_of((z * 2 + swap(half)) * size, size), size)
        value = jnp.concatenate([g[0, rows, :], g[1, rows, :]], axis=1)
        g_ref[half] = value
        if second:
            sums = [sums[0] + fold(g0_ref[half] * value), sums[1] + fold(value * value)]
        else:
            sums = [sums[0] + fold(value * value), sums[1]]
        rows = pl.ds(pl.multiple_of(swap(half) * size, size), size)
        s_ref[half] = jnp.concatenate([s[0, rows, :], s[1, rows, :]], axis=1).astype(BF)
    sum_ref[...] = jnp.concatenate(sums + [jnp.zeros((6, 128), F32)], axis=0)


def window(place, blocks, constants, *more):
    return pl.pallas_call(
        lambda *refs: window_kernel(len(more) > 0, *refs),
        in_specs=[SMEM] + [VMEM] * (9 + len(more)),
        out_specs=[VMEM, VMEM, VMEM],
        out_shape=[
            jax.ShapeDtypeStruct((2, 8 * CC, 256), F32),
            jax.ShapeDtypeStruct((2, 8 * CC, 256), BF),
            jax.ShapeDtypeStruct((8, 128), F32),
        ],
        scratch_shapes=[pltpu.VMEM((2, 64 * CC, 128), F32)] * 2
        + [pltpu.VMEM((2, 16 * CC, 128), F32)],
        compiler_params=params(12),
        cost_estimate=cost(1 << 30),
        name="window",
    )(place, *blocks, *constants, *more)


def last_kernel(
    place_ref, sum_ref, i0a, i0b, i1a, i1b, data_ref, g0, g0_got, h, h_got, model_ref, res_ref
):
    core = place_ref[1]
    sums = jnp.sum(sum_ref[...], axis=1, keepdims=True)
    gg, gh, hh, ii, ij, jj = [sums[k : k + 1] for k in range(6)]
    alpha0 = gg / ii
    fresh = gg - 2.0 * alpha0 * gh + alpha0 * alpha0 * hh
    stay = 1.0 + fresh / gg
    delta = stay * stay * ii - 2.0 * stay * alpha0 * ij + alpha0 * alpha0 * jj
    alpha1 = fresh / delta
    on_first = alpha0 + alpha1 * stay
    on_second = alpha1 * alpha0
    for half in range(2):
        at = pl.ds(pl.multiple_of((half + core - 2 * half * core) * 16, 16), 16)
        for f in range(4):
            for p in range(2):
                rows = slice(f * 32 + p * 16, f * 32 + p * 16 + 16)
                left = g0[0, rows, :] if half == 0 else g0_got[rows, :]
                right = h[0, rows, :] if half == 0 else h_got[rows, :]
                model_ref[p, f, at, :] = on_first * left - on_second * right
                rows = slice(half * 32 + p * 16, half * 32 + p * 16 + 16)
                i0, i1 = ((i0a, i1a), (i0b, i1b))[f // 2]
                change = on_first * i0[f % 2, rows, :] - on_second * i1[f % 2, rows, :]
                res_ref[p, f, at, :] = data_ref[p, f, at, :] - change


def last(place, *arrays):
    shape = jax.ShapeDtypeStruct((2, 4, 32, 256), F32)
    return pl.pallas_call(
        last_kernel,
        in_specs=[SMEM] + [VMEM] * len(arrays),
        out_specs=[VMEM, VMEM],
        out_shape=[shape, shape],
        compiler_params=params(8),
        cost_estimate=cost(1 << 20),
        name="last",
    )(place, *arrays)


def total(values):
    values = values + move(values, other_core)
    for axis in (along_z, along_small, along_big):
        values = values + move(values, axis(1)) + move(values, axis(2)) + move(values, axis(3))
    return values


def body(kernel, data, cutoffs):
    rcv = lax.axis_index("rcv")
    freq = lax.axis_index("freq")
    yy, xx, zz, core = rcv // 4, rcv % 4, freq // 2, freq % 2
    place = jnp.stack([zz, core]).astype(jnp.int32)
    far = jnp.arange(16, dtype=jnp.int32) // 4
    near = jnp.arange(16, dtype=jnp.int32) % 4
    off_y = jnp.where(core == 0, far, near)
    off_x = jnp.where(core == 0, near, far)
    table = (yy + off_y) % 4 * 4 + (xx + off_x) % 4

    matrix = window_matrix()
    high = matrix.astype(jnp.bfloat16)
    low = (matrix - high.astype(np.float32)).astype(jnp.bfloat16)
    stacked = jnp.asarray(np.concatenate([high, low, high], axis=1))
    own_rows = stacked.reshape(2, 4, 8, 192).swapaxes(0, 1).reshape(4, 16, 192)
    bins = jnp.arange(1, F + 1, dtype=jnp.int32)
    phase = (bins[:, None] * cutoffs[None, :] % NT).astype(F32) * (2.0 * math.pi / NT)
    share = (cutoffs.astype(F32) / NT)[None, :]
    constants = (stacked, own_rows, jnp.cos(phase), jnp.sin(phase), share)

    def summed(parts):
        out = parts[0].astype(F32)
        for part in parts[1:]:
            out = out + part.astype(F32)
        return out.astype(BF)

    def sum_big(own):
        got = [move(own[kb], along_big(kb)) for kb in (2, 1, 3)]
        return [summed([own[0][ks]] + [part[ks] for part in got]) for ks in range(4)]

    def gather_terms(row):
        mine = summed([row[0]] + [move(row[ks], along_small(ks)) for ks in (2, 1, 3)])
        mine = mine.reshape(4, 2, 32, 256)
        mine = jnp.stack([mine[:, 0], move(mine[:, 1], other_core)]).reshape(256, 256)
        return [mine] + [move(mine, along_z(-k)) for k in (1, 2, 3)]

    def image_of(shaped, i0=(None, None), early=()):
        shaped = shaped.reshape(2, 4, 32, 256)
        shaped = jnp.stack([shaped[0], move(shaped[1], other_core)], axis=1).reshape(4, 64, 256)
        row = [shaped] + [move(shaped, along_small(-ks)) for ks in (1, 2, 3)]
        one, two = [jnp.stack([part[k : k + 2] for part in row]) for k in (0, 2)]
        near = [move(one, along_big(-kb)) for kb in (1, 3)]
        far = move(one, along_big(-2))
        (out,) = forward((0,), table, turned[0], [one])
        two, out = lax.optimization_barrier((two, out))
        near_two = [move(two, along_big(-kb)) for kb in (1, 3)]
        far_two = move(two, along_big(-2))
        (out_two,) = forward((0,), table, turned[1], [two])
        out, sums = forward((1, 3, 2), table, turned[0], near + [far], out, True, i0[0])
        out_two, out = lax.optimization_barrier((out_two, out))
        (out_two,) = forward((1, 3), table, turned[1], near_two, out_two)
        if early:
            early = (*early, sums)
        out_two, sums_two = forward(
            (2,), table, turned[1], [far_two], out_two, True, i0[1], early
        )
        return (out, out_two), (sums, sums_two)

    start = jnp.swapaxes(data, 2, 3)
    out = first_adjoint(place, table, start, kernel)
    big = [pltpu.with_memory_space_constraint(t, pltpu.VMEM) for t in out[:4]]
    held, turned, own = big[:2], big[2:], out[4:]
    g0, s0, gg = window(place, gather_terms(sum_big(own)), constants)
    i0, ii = image_of(s0)
    rows = [lax.optimization_barrier(sum_big(adjoint(table, i0[k], held[k]))) for k in range(2)]
    rows = [jnp.concatenate(pair) for pair in zip(*rows)]
    h, s1, hh = window(place, gather_terms(rows), constants, g0)
    i1, sums = image_of(s1, i0, (gg, hh, *ii))
    g0_got = move(g0[1], other_core)
    h_got = move(h[1], other_core)
    model, residual = last(
        place, total(sums[1]), *i0, *i1, start, g0, g0_got, h, h_got
    )
    return jnp.swapaxes(model, 2, 3), jnp.swapaxes(residual, 2, 3)


def solution(mesh):
    placed = P(None, "freq", "rcv", None)
    return jax.shard_map(
        body,
        mesh=mesh,
        in_specs=(placed, placed, P("rcv")),
        out_specs=(placed, placed),
        check_vma=False,
    )
```

```python
import math

import jax
import jax.numpy as jnp
import numpy as np
from jax import lax
from jax.experimental import pallas as pl
from jax.experimental.pallas import tpu as pltpu
from jax.sharding import PartitionSpec as P

NT = 1024
F = 32
AXES = ("rcv", "freq")
OFFSETS = (0, 2, 1, 3)
BF = jnp.bfloat16
F32 = jnp.float32
VMEM = pl.BlockSpec(memory_space=pltpu.VMEM)
HBM = pl.BlockSpec(memory_space=pltpu.HBM)
CC = 16
SMEM = pl.BlockSpec(memory_space=pltpu.SMEM)
NT_DIMS = (((1,), (1,)), ((), ()))


def index(y, x, z, c):
    return (y * 4 + x) * 8 + z * 2 + c


DEVICES = [(y, x, z, c) for y in range(4) for x in range(4) for z in range(4) for c in range(2)]


def move(value, target):
    pairs = [(index(*d), index(*target(*d))) for d in DEVICES]
    return lax.ppermute(value, AXES, pairs)


def along_big(step):
    def target(y, x, z, c):
        return ((y + step) % 4, x, z, c) if c == 0 else (y, (x + step) % 4, z, c)

    return target


def along_small(step):
    def target(y, x, z, c):
        return (y, (x + step) % 4, z, c) if c == 0 else ((y + step) % 4, x, z, c)

    return target


def along_z(step):
    return lambda y, x, z, c: (y, x, (z + step) % 4, c)


def other_core(y, x, z, c):
    return (y, x, z, 1 - c)


def window_matrix():
    bins = np.arange(1, F + 1)
    theta = 2.0 * np.pi / NT

    def ratio(k):
        half = theta * k / 2.0
        safe = np.where(k == 0, 1.0, half)
        return np.where(k == 0, 0.0, 0.5 - 0.5j / np.tan(safe))

    direct = ratio(bins[:, None] - bins[None, :]) / NT
    mirror = ratio(bins[:, None] + bins[None, :]) / NT
    top = np.concatenate([direct.real + mirror.real, -direct.imag + mirror.imag], axis=1)
    low = np.concatenate([direct.imag + mirror.imag, direct.real - mirror.real], axis=1)
    return np.concatenate([top, low], axis=0).astype(np.float32)


def cost(flops):
    return pl.CostEstimate(flops=flops, bytes_accessed=4 << 20, transcendentals=0)


def params(mib):
    return pltpu.CompilerParams(vmem_limit_bytes=mib << 20)


def swapped(v, sign):
    rows = []
    for k in range(0, 64, 32):
        rows += [sign * v[k + 16 : k + 32], -sign * v[k : k + 16]]
    return jnp.concatenate(rows, axis=0)


def terms(kb, f, u, at, j_ref, k_ref, out_ref):
    v = swapped(u, 1)
    for ks in range(4):
        cols = pl.ds(pl.multiple_of(j_ref[kb * 4 + ks] * 256, 256), 256)
        r = jnp.dot(u, k_ref[0, f, :, cols], preferred_element_type=F32)
        r = r + jnp.dot(v, k_ref[1, f, :, cols], preferred_element_type=F32)
        out_ref[ks, at] = r.astype(BF)


def first_kernel(place_ref, j_ref, data_hbm, k_hbm, *refs):
    held_refs, turned_refs, out_refs = refs[:2], refs[2:4], refs[4:8]
    data_ref, sem, sems = refs[8:]
    core = place_ref[1]
    fetch = pltpu.make_async_copy(data_hbm, data_ref, sem)
    fetch.start()
    copies = [
        [
            pltpu.make_async_copy(k_hbm.at[p, f], held_refs[f // 2].at[p, f % 2], sems.at[p, f])
            for p in range(2)
        ]
        for f in range(4)
    ]
    for f in range(2):
        for p in range(2):
            copies[f][p].start()
    fetch.wait()
    for f in range(4):
        rows = []
        for half in range(2):
            at = pl.ds(pl.multiple_of((half + core - 2 * half * core) * 16, 16), 16)
            rows += [data_ref[0, f, at, :], data_ref[1, f, at, :]]
        u = jnp.concatenate(rows, axis=0).astype(BF)
        for p in range(2):
            copies[f][p].wait()
            if f < 2:
                copies[f + 2][p].start()
        for kb in range(4):
            k_ref = held_refs[f // 2]
            terms(kb, f % 2, u, f, j_ref, k_ref, out_refs[kb])
            for p in range(2):
                for j in range(kb * 4, kb * 4 + 4):
                    at = slice(j * 256, j * 256 + 256)
                    turned_refs[f // 2][p, f % 2, at, :] = k_ref[p, f % 2, :, at].T


def first_adjoint(place, table, data, kernel):
    return pl.pallas_call(
        first_kernel,
        in_specs=[SMEM, SMEM, HBM, HBM],
        out_specs=[VMEM] * 8,
        out_shape=[pltpu.VMEM((2, 2, 256, 4096), BF)] * 2
        + [pltpu.VMEM((2, 2, 4096, 256), BF)] * 2
        + [jax.ShapeDtypeStruct((4, 4, 64, 256), BF)] * 4,
        scratch_shapes=[
            pltpu.VMEM(data.shape, F32),
            pltpu.SemaphoreType.DMA,
            pltpu.SemaphoreType.DMA((2, 4)),
        ],
        compiler_params=params(8),
        cost_estimate=cost(1 << 33),
        name="first_adjoint",
    )(
        place,
        table,
        pltpu.with_memory_space_constraint(data, pltpu.HBM),
        pltpu.with_memory_space_constraint(kernel, pltpu.HBM),
    )


TERMS = jax.ShapeDtypeStruct((4, 2, 64, 256), BF)


def adjoint_kernel(j_ref, u_ref, k_ref, *out_refs):
    for f in range(2):
        u = u_ref[f].astype(BF)
        for kb in (2, 1, 3, 0):
            terms(kb, f, u, f, j_ref, k_ref, out_refs[kb])


def adjoint(table, u, kernel):
    return pl.pallas_call(
        adjoint_kernel,
        in_specs=[SMEM, VMEM, VMEM],
        out_specs=[VMEM] * 4,
        out_shape=[TERMS] * 4,
        compiler_params=params(8),
        cost_estimate=cost(1 << 31),
        name="adjoint",
    )(table, u, kernel)


def fold(v):
    v = jnp.sum(v, axis=0, keepdims=True)
    return v[:, :128] + v[:, 128:]


def forward_kernel(kbs, first, last, second, early, j_ref, k_ref, *refs):
    x_refs, refs = refs[: len(kbs)], refs[len(kbs) :]
    if not first:
        before_ref, *refs = refs
    if second:
        i0_ref, *refs = refs
    early_refs, refs = refs[:early], refs[early:]
    out_ref = refs[0]

    zero = jnp.zeros((1, 128), F32)
    sums = [zero, zero]
    for f in range(2):
        out = jnp.zeros((64, 256), F32) if first else before_ref[f]
        for kb, x_ref in zip(kbs, x_refs):
            for ks in range(4):
                rows = pl.ds(pl.multiple_of(j_ref[kb * 4 + ks] * 256, 256), 256)
                x = x_ref[ks, f]
                out = out + jnp.dot(x, k_ref[0, f, rows, :], preferred_element_type=F32)
                out = out + jnp.dot(
                    swapped(x, -1), k_ref[1, f, rows, :], preferred_element_type=F32
                )
        out_ref[f] = out
        if second:
            sums[0] = sums[0] + fold(i0_ref[f] * out)
        if last:
            sums[1] = sums[1] + fold(out * out)
    if early:
        gg, hh, ii0, ii1, other = [ref[...] for ref in early_refs]
        rows = [gg[0:1], hh[0:2], ii0[1:2] + ii1[1:2]]
        rows += [other[0:1] + sums[0], other[1:2] + sums[1], zero, zero]
        refs[1][...] = jnp.concatenate(rows, axis=0)
    elif last:
        refs[1][...] = jnp.concatenate(sums + [jnp.zeros((6, 128), F32)], axis=0)


def forward(kbs, table, kernel, blocks, before=None, last=False, i0=None, early=()):
    inputs = [kernel, *blocks]
    inputs += [a for a in (before, i0) if a is not None] + list(early)
    out = [jax.ShapeDtypeStruct((2, 64, 256), F32)]
    if last:
        out.append(jax.ShapeDtypeStruct((8, 128), F32))
    flags = (kbs, before is None, last, i0 is not None, len(early))
    return pl.pallas_call(
        lambda *refs: forward_kernel(*flags, *refs),
        in_specs=[SMEM] + [VMEM] * len(inputs),
        out_specs=[VMEM] * len(out),
        out_shape=out,
        compiler_params=params(8),
        cost_estimate=cost(1 << 31),
        name="forward",
    )(table, *inputs)


def parts_of(x):
    high = x.astype(BF)
    low = (x - high.astype(F32)).astype(BF)
    return jnp.concatenate([high, high, low], axis=0)


def window_kernel(second, place_ref, a0, a1, a2, a3, m_ref, mo_ref, cos_ref, sin_ref, n_ref, *refs):
    if second:
        g0_ref, g_ref, s_ref, sum_ref, y, g, s = refs
    else:
        g_ref, s_ref, sum_ref, y, g, s = refs
    z = place_ref[0]
    core = place_ref[1]

    size = 8 * CC

    def swap(half):
        return half + core - 2 * half * core

    for k, a in zip(OFFSETS, (a0, a1, a2, a3)):
        for half in range(2):
            at = (lax.rem(z + k, 4) * 2 + swap(half)) * size
            rows = pl.ds(pl.multiple_of(at, size), size)
            part = a[pl.ds(half * size, size), :].astype(F32)
            y[0, rows, :] = part[:, :128]
            y[1, rows, :] = part[:, 128:]

    cos = cos_ref[...]
    sin = sin_ref[...]
    share = n_ref[...]
    eight = pl.ds(pl.multiple_of(z * 8, 8), 8)
    cos_own = cos_ref[eight, :]
    sin_own = sin_ref[eight, :]

    def take(ref, first, count):
        rows = pl.ds(first, count, stride=2 * CC)
        return jnp.concatenate([ref[0, rows, :], ref[1, rows, :]], axis=1)

    def put(ref, first, value):
        rows = pl.ds(first, value.shape[0], stride=2 * CC)
        ref[0, rows, :] = value[:, :128]
        ref[1, rows, :] = value[:, 128:]

    def products(matrix, pairs):
        columns = []
        for re, im in pairs:
            columns.append(parts_of(jnp.concatenate([re, im], axis=0)))
            turned = jnp.concatenate([cos * re - sin * im, sin * re + cos * im], axis=0)
            columns.append(parts_of(turned))
        return jnp.dot(matrix, jnp.concatenate(columns, axis=1), preferred_element_type=F32)

    def combine(re, im, both, at, c, d):
        n = re.shape[0]
        plain = both[:, at * 512 : at * 512 + 256]
        w = both[:, at * 512 + 256 : at * 512 + 512]
        out_re = share * re + plain[:n] - c * w[:n] - d * w[n:]
        out_im = share * im + plain[n:] - c * w[n:] + d * w[:n]
        return out_re, out_im

    def four(step, carry):
        first = step * 4
        pairs = [(take(y, first + i, F), take(y, first + i + CC, F)) for i in range(4)]
        both = products(m_ref[...], pairs)
        grads = []
        for i, (re, im) in enumerate(pairs):
            re, im = combine(re, im, both, i, cos, sin)
            put(g, first + i, re)
            put(g, first + i + CC, im)
            grads.append((re, im))
        both = products(mo_ref[z], grads)
        for i in range(4):
            re = take(g, z * 2 * size + first + i, 8)
            im = take(g, z * 2 * size + first + i + CC, 8)
            re, im = combine(re, im, both, i, cos_own, sin_own)
            put(s, first + i, re)
            put(s, first + i + CC, im)
        return carry

    lax.fori_loop(0, CC // 4, four, 0)
    sums = [jnp.zeros((1, 128), F32)] * 2
    for half in range(2):
        rows = pl.ds(pl.multiple_of((z * 2 + swap(half)) * size, size), size)
        value = jnp.concatenate([g[0, rows, :], g[1, rows, :]], axis=1)
        g_ref[half] = value
        if second:
            sums = [sums[0] + fold(g0_ref[half] * value), sums[1] + fold(value * value)]
        else:
            sums = [sums[0] + fold(value * value), sums[1]]
        rows = pl.ds(pl.multiple_of(swap(half) * size, size), size)
        s_ref[half] = jnp.concatenate([s[0, rows, :], s[1, rows, :]], axis=1).astype(BF)
    sum_ref[...] = jnp.concatenate(sums + [jnp.zeros((6, 128), F32)], axis=0)


def window(place, blocks, constants, *more):
    return pl.pallas_call(
        lambda *refs: window_kernel(len(more) > 0, *refs),
        in_specs=[SMEM] + [VMEM] * (9 + len(more)),
        out_specs=[VMEM, VMEM, VMEM],
        out_shape=[
            jax.ShapeDtypeStruct((2, 8 * CC, 256), F32),
            jax.ShapeDtypeStruct((2, 8 * CC, 256), BF),
            jax.ShapeDtypeStruct((8, 128), F32),
        ],
        scratch_shapes=[pltpu.VMEM((2, 64 * CC, 128), F32)] * 2
        + [pltpu.VMEM((2, 16 * CC, 128), F32)],
        compiler_params=params(12),
        cost_estimate=cost(1 << 30),
        name="window",
    )(place, *blocks, *constants, *more)


def last_kernel(
    place_ref, sum_ref, i0a, i0b, i1a, i1b, data_ref, g0, g0_got, h, h_got, model_ref, res_ref
):
    core = place_ref[1]
    sums = jnp.sum(sum_ref[...], axis=1, keepdims=True)
    gg, gh, hh, ii, ij, jj = [sums[k : k + 1] for k in range(6)]
    alpha0 = gg / ii
    fresh = gg - 2.0 * alpha0 * gh + alpha0 * alpha0 * hh
    stay = 1.0 + fresh / gg
    delta = stay * stay * ii - 2.0 * stay * alpha0 * ij + alpha0 * alpha0 * jj
    alpha1 = fresh / delta
    on_first = alpha0 + alpha1 * stay
    on_second = alpha1 * alpha0
    for half in range(2):
        at = pl.ds(pl.multiple_of((half + core - 2 * half * core) * 16, 16), 16)
        for f in range(4):
            for p in range(2):
                rows = slice(f * 32 + p * 16, f * 32 + p * 16 + 16)
                left = g0[0, rows, :] if half == 0 else g0_got[rows, :]
                right = h[0, rows, :] if half == 0 else h_got[rows, :]
                model_ref[p, f, at, :] = on_first * left - on_second * right
                rows = slice(half * 32 + p * 16, half * 32 + p * 16 + 16)
                i0, i1 = ((i0a, i1a), (i0b, i1b))[f // 2]
                change = on_first * i0[f % 2, rows, :] - on_second * i1[f % 2, rows, :]
                res_ref[p, f, at, :] = data_ref[p, f, at, :] - change


def last(place, *arrays):
    shape = jax.ShapeDtypeStruct((2, 4, 32, 256), F32)
    return pl.pallas_call(
        last_kernel,
        in_specs=[SMEM] + [VMEM] * len(arrays),
        out_specs=[VMEM, VMEM],
        out_shape=[shape, shape],
        compiler_params=params(8),
        cost_estimate=cost(1 << 20),
        name="last",
    )(place, *arrays)


def total(values):
    values = values + move(values, other_core)
    for axis in (along_z, along_small, along_big):
        values = values + move(values, axis(2)) + move(values, axis(1)) + move(values, axis(3))
    return values


def body(kernel, data, cutoffs):
    rcv = lax.axis_index("rcv")
    freq = lax.axis_index("freq")
    yy, xx, zz, core = rcv // 4, rcv % 4, freq // 2, freq % 2
    place = jnp.stack([zz, core]).astype(jnp.int32)
    far = jnp.arange(16, dtype=jnp.int32) // 4
    near = jnp.asarray(np.array(OFFSETS * 4, np.int32))
    off_y = jnp.where(core == 0, far, near)
    off_x = jnp.where(core == 0, near, far)
    table = (yy + off_y) % 4 * 4 + (xx + off_x) % 4

    matrix = window_matrix()
    high = matrix.astype(jnp.bfloat16)
    low = (matrix - high.astype(np.float32)).astype(jnp.bfloat16)
    stacked = jnp.asarray(np.concatenate([high, low, high], axis=1))
    own_rows = stacked.reshape(2, 4, 8, 192).swapaxes(0, 1).reshape(4, 16, 192)
    bins = jnp.arange(1, F + 1, dtype=jnp.int32)
    phase = (bins[:, None] * cutoffs[None, :] % NT).astype(F32) * (2.0 * math.pi / NT)
    share = (cutoffs.astype(F32) / NT)[None, :]
    constants = (stacked, own_rows, jnp.cos(phase), jnp.sin(phase), share)

    def summed(parts):
        out = parts[0].astype(F32)
        for part in parts[1:]:
            out = out + part.astype(F32)
        return out.astype(BF)

    def sum_big(own):
        got = [move(own[kb], along_big(kb)) for kb in (2, 1, 3)]
        return [summed([own[0][ks]] + [part[ks] for part in got]) for ks in range(4)]

    def gather_terms(row):
        mine = summed([row[0]] + [move(row[n], along_small(OFFSETS[n])) for n in (1, 2, 3)])
        mine = mine.reshape(4, 2, 32, 256)
        mine = jnp.stack([mine[:, 0], move(mine[:, 1], other_core)]).reshape(256, 256)
        return [mine] + [move(mine, along_z(-k)) for k in OFFSETS[1:]]

    def image_of(shaped, i0=(None, None), early=()):
        shaped = shaped.reshape(2, 4, 32, 256)
        shaped = jnp.stack([shaped[0], move(shaped[1], other_core)], axis=1).reshape(4, 64, 256)
        row = [shaped] + [move(shaped, along_small(-ks)) for ks in OFFSETS[1:]]
        one, two = [jnp.stack([part[k : k + 2] for part in row]) for k in (0, 2)]
        near = [move(one, along_big(-kb)) for kb in (1, 3)]
        far = move(one, along_big(-2))
        (out,) = forward((0,), table, turned[0], [one])
        two, out = lax.optimization_barrier((two, out))
        near_two = [move(two, along_big(-kb)) for kb in (1, 3)]
        far_two = move(two, along_big(-2))
        (out_two,) = forward((0,), table, turned[1], [two])
        out, sums = forward((1, 3, 2), table, turned[0], near + [far], out, True, i0[0])
        out_two, out = lax.optimization_barrier((out_two, out))
        if early:
            early = (*early, sums)
            (out_two,) = forward((1, 3), table, turned[1], near_two, out_two)
            kbs, blocks = (2,), [far_two]
        else:
            kbs, blocks = (1, 3, 2), [*near_two, far_two]
        out_two, sums_two = forward(kbs, table, turned[1], blocks, out_two, True, i0[1], early)
        return (out, out_two), (sums, sums_two)

    start = jnp.swapaxes(data, 2, 3)
    out = first_adjoint(place, table, start, kernel)
    big = [pltpu.with_memory_space_constraint(t, pltpu.VMEM) for t in out[:4]]
    held, turned, own = big[:2], big[2:], out[4:]
    g0, s0, gg = window(place, gather_terms(sum_big(own)), constants)
    i0, ii = image_of(s0)
    rows = [lax.optimization_barrier(sum_big(adjoint(table, i0[k], held[k]))) for k in range(2)]
    rows = [jnp.concatenate(pair) for pair in zip(*rows)]
    h, s1, hh = window(place, gather_terms(rows), constants, g0)
    i1, sums = image_of(s1, i0, (gg, hh, *ii))
    g0_got = move(g0[1], other_core)
    h_got = move(h[1], other_core)
    model, residual = last(
        place, total(sums[1]), *i0, *i1, start, g0, g0_got, h, h_got
    )
    return jnp.swapaxes(model, 2, 3), jnp.swapaxes(residual, 2, 3)


def solution(mesh):
    placed = P(None, "freq", "rcv", None)
    return jax.shard_map(
        body,
        mesh=mesh,
        in_specs=(placed, placed, P("rcv")),
        out_specs=(placed, placed),
        check_vma=False,
    )
```

```python
import math

import jax
import jax.numpy as jnp
import numpy as np
from jax import lax
from jax.experimental import pallas as pl
from jax.experimental.pallas import tpu as pltpu
from jax.sharding import PartitionSpec as P

NT = 1024
F = 32
AXES = ("rcv", "freq")
OFFSETS = (0, 2, 1, 3)
BF = jnp.bfloat16
F32 = jnp.float32
VMEM = pl.BlockSpec(memory_space=pltpu.VMEM)
HBM = pl.BlockSpec(memory_space=pltpu.HBM)
CC = 16
SMEM = pl.BlockSpec(memory_space=pltpu.SMEM)
NT_DIMS = (((1,), (1,)), ((), ()))


def index(y, x, z, c):
    return (y * 4 + x) * 8 + z * 2 + c


DEVICES = [(y, x, z, c) for y in range(4) for x in range(4) for z in range(4) for c in range(2)]


def move(value, target):
    pairs = [(index(*d), index(*target(*d))) for d in DEVICES]
    return lax.ppermute(value, AXES, pairs)


def along_big(step):
    def target(y, x, z, c):
        return ((y + step) % 4, x, z, c) if c == 0 else (y, (x + step) % 4, z, c)

    return target


def along_small(step):
    def target(y, x, z, c):
        return (y, (x + step) % 4, z, c) if c == 0 else ((y + step) % 4, x, z, c)

    return target


def along_z(step):
    return lambda y, x, z, c: (y, x, (z + step) % 4, c)


def other_core(y, x, z, c):
    return (y, x, z, 1 - c)


def window_matrix():
    bins = np.arange(1, F + 1)
    theta = 2.0 * np.pi / NT

    def ratio(k):
        half = theta * k / 2.0
        safe = np.where(k == 0, 1.0, half)
        return np.where(k == 0, 0.0, 0.5 - 0.5j / np.tan(safe))

    direct = ratio(bins[:, None] - bins[None, :]) / NT
    mirror = ratio(bins[:, None] + bins[None, :]) / NT
    top = np.concatenate([direct.real + mirror.real, -direct.imag + mirror.imag], axis=1)
    low = np.concatenate([direct.imag + mirror.imag, direct.real - mirror.real], axis=1)
    return np.concatenate([top, low], axis=0).astype(np.float32)


def cost(flops):
    return pl.CostEstimate(flops=flops, bytes_accessed=4 << 20, transcendentals=0)


def params(mib):
    return pltpu.CompilerParams(vmem_limit_bytes=mib << 20)


def swapped(v, sign):
    rows = []
    for k in range(0, 64, 32):
        rows += [sign * v[k + 16 : k + 32], -sign * v[k : k + 16]]
    return jnp.concatenate(rows, axis=0)


def terms(kb, f, u, at, j_ref, k_ref, out_ref):
    v = swapped(u, 1)
    for ks in range(4):
        cols = pl.ds(pl.multiple_of(j_ref[kb * 4 + ks] * 256, 256), 256)
        r = jnp.dot(u, k_ref[0, f, :, cols], preferred_element_type=F32)
        r = r + jnp.dot(v, k_ref[1, f, :, cols], preferred_element_type=F32)
        out_ref[ks, at] = r.astype(BF)


def first_kernel(place_ref, j_ref, data_hbm, k_hbm, *refs):
    held_refs, turned_refs, out_refs = refs[:2], refs[2:4], refs[4:8]
    data_ref, sem, sems = refs[8:]
    core = place_ref[1]
    fetch = pltpu.make_async_copy(data_hbm, data_ref, sem)
    fetch.start()
    copies = [
        [
            pltpu.make_async_copy(k_hbm.at[p, f], held_refs[f // 2].at[p, f % 2], sems.at[p, f])
            for p in range(2)
        ]
        for f in range(4)
    ]
    for f in range(2):
        for p in range(2):
            copies[f][p].start()
    fetch.wait()
    for f in range(4):
        rows = []
        for half in range(2):
            at = pl.ds(pl.multiple_of((half + core - 2 * half * core) * 16, 16), 16)
            rows += [data_ref[0, f, at, :], data_ref[1, f, at, :]]
        u = jnp.concatenate(rows, axis=0).astype(BF)
        for p in range(2):
            copies[f][p].wait()
            if f < 2:
                copies[f + 2][p].start()
        for kb in range(4):
            k_ref = held_refs[f // 2]
            terms(kb, f % 2, u, f, j_ref, k_ref, out_refs[kb])
            for p in range(2):
                for j in range(kb * 4, kb * 4 + 4):
                    at = slice(j * 256, j * 256 + 256)
                    turned_refs[f // 2][p, f % 2, at, :] = k_ref[p, f % 2, :, at].T


def first_adjoint(place, table, data, kernel):
    return pl.pallas_call(
        first_kernel,
        in_specs=[SMEM, SMEM, HBM, HBM],
        out_specs=[VMEM] * 8,
        out_shape=[pltpu.VMEM((2, 2, 256, 4096), BF)] * 2
        + [pltpu.VMEM((2, 2, 4096, 256), BF)] * 2
        + [jax.ShapeDtypeStruct((4, 4, 64, 256), BF)] * 4,
        scratch_shapes=[
            pltpu.VMEM(data.shape, F32),
            pltpu.SemaphoreType.DMA,
            pltpu.SemaphoreType.DMA((2, 4)),
        ],
        compiler_params=params(8),
        cost_estimate=cost(1 << 33),
        name="first_adjoint",
    )(
        place,
        table,
        pltpu.with_memory_space_constraint(data, pltpu.HBM),
        pltpu.with_memory_space_constraint(kernel, pltpu.HBM),
    )


TERMS = jax.ShapeDtypeStruct((4, 2, 64, 256), BF)


def adjoint_kernel(j_ref, u_ref, k_ref, *out_refs):
    for f in range(2):
        u = u_ref[f].astype(BF)
        for kb in (2, 1, 3, 0):
            terms(kb, f, u, f, j_ref, k_ref, out_refs[kb])


def adjoint(table, u, kernel):
    return pl.pallas_call(
        adjoint_kernel,
        in_specs=[SMEM, VMEM, VMEM],
        out_specs=[VMEM] * 4,
        out_shape=[TERMS] * 4,
        compiler_params=params(8),
        cost_estimate=cost(1 << 31),
        name="adjoint",
    )(table, u, kernel)


def fold(v):
    v = jnp.sum(v, axis=0, keepdims=True)
    return v[:, :128] + v[:, 128:]


def forward_kernel(kbs, first, last, second, early, j_ref, k_ref, *refs):
    x_refs, refs = refs[: len(kbs)], refs[len(kbs) :]
    if not first:
        before_ref, *refs = refs
    if second:
        i0_ref, *refs = refs
    early_refs, refs = refs[:early], refs[early:]
    out_ref = refs[0]

    zero = jnp.zeros((1, 128), F32)
    sums = [zero, zero]
    for f in range(2):
        out = jnp.zeros((64, 256), F32) if first else before_ref[f]
        for kb, x_ref in zip(kbs, x_refs):
            for ks in range(4):
                rows = pl.ds(pl.multiple_of(j_ref[kb * 4 + ks] * 256, 256), 256)
                x = x_ref[ks, f]
                out = out + jnp.dot(x, k_ref[0, f, rows, :], preferred_element_type=F32)
                out = out + jnp.dot(
                    swapped(x, -1), k_ref[1, f, rows, :], preferred_element_type=F32
                )
        out_ref[f] = out
        if second:
            sums[0] = sums[0] + fold(i0_ref[f] * out)
        if last:
            sums[1] = sums[1] + fold(out * out)
    if early:
        gg, hh, ii0, ii1, other = [ref[...] for ref in early_refs]
        rows = [gg[0:1], hh[0:2], ii0[1:2] + ii1[1:2]]
        rows += [other[0:1] + sums[0], other[1:2] + sums[1], zero, zero]
        refs[1][...] = jnp.concatenate(rows, axis=0)
    elif last:
        refs[1][...] = jnp.concatenate(sums + [jnp.zeros((6, 128), F32)], axis=0)


def forward(kbs, table, kernel, blocks, before=None, last=False, i0=None, early=()):
    inputs = [kernel, *blocks]
    inputs += [a for a in (before, i0) if a is not None] + list(early)
    out = [jax.ShapeDtypeStruct((2, 64, 256), F32)]
    if last:
        out.append(jax.ShapeDtypeStruct((8, 128), F32))
    flags = (kbs, before is None, last, i0 is not None, len(early))
    return pl.pallas_call(
        lambda *refs: forward_kernel(*flags, *refs),
        in_specs=[SMEM] + [VMEM] * len(inputs),
        out_specs=[VMEM] * len(out),
        out_shape=out,
        compiler_params=params(8),
        cost_estimate=cost(1 << 31),
        name="forward",
    )(table, *inputs)


def parts_of(x):
    high = x.astype(BF)
    low = (x - high.astype(F32)).astype(BF)
    return jnp.concatenate([high, high, low], axis=0)


def window_kernel(second, place_ref, a0, a1, a2, a3, m_ref, mo_ref, cos_ref, sin_ref, n_ref, *refs):
    if second:
        g0_ref, g_ref, s_ref, sum_ref, y, g, s = refs
    else:
        g_ref, s_ref, sum_ref, y, g, s = refs
    z = place_ref[0]
    core = place_ref[1]

    size = 8 * CC

    def swap(half):
        return half + core - 2 * half * core

    for k, a in zip(OFFSETS, (a0, a1, a2, a3)):
        for half in range(2):
            at = (lax.rem(z + k, 4) * 2 + swap(half)) * size
            rows = pl.ds(pl.multiple_of(at, size), size)
            part = a[pl.ds(half * size, size), :].astype(F32)
            y[0, rows, :] = part[:, :128]
            y[1, rows, :] = part[:, 128:]

    cos = cos_ref[...]
    sin = sin_ref[...]
    share = n_ref[...]
    eight = pl.ds(pl.multiple_of(z * 8, 8), 8)
    cos_own = cos_ref[eight, :]
    sin_own = sin_ref[eight, :]

    def take(ref, first, count):
        rows = pl.ds(first, count, stride=2 * CC)
        return jnp.concatenate([ref[0, rows, :], ref[1, rows, :]], axis=1)

    def put(ref, first, value):
        rows = pl.ds(first, value.shape[0], stride=2 * CC)
        ref[0, rows, :] = value[:, :128]
        ref[1, rows, :] = value[:, 128:]

    def products(matrix, pairs):
        columns = []
        for re, im in pairs:
            columns.append(parts_of(jnp.concatenate([re, im], axis=0)))
            turned = jnp.concatenate([cos * re - sin * im, sin * re + cos * im], axis=0)
            columns.append(parts_of(turned))
        return jnp.dot(matrix, jnp.concatenate(columns, axis=1), preferred_element_type=F32)

    def combine(re, im, both, at, c, d):
        n = re.shape[0]
        plain = both[:, at * 512 : at * 512 + 256]
        w = both[:, at * 512 + 256 : at * 512 + 512]
        out_re = share * re + plain[:n] - c * w[:n] - d * w[n:]
        out_im = share * im + plain[n:] - c * w[n:] + d * w[:n]
        return out_re, out_im

    def four(step, carry):
        first = step * 4
        pairs = [(take(y, first + i, F), take(y, first + i + CC, F)) for i in range(4)]
        both = products(m_ref[...], pairs)
        grads = []
        for i, (re, im) in enumerate(pairs):
            re, im = combine(re, im, both, i, cos, sin)
            put(g, first + i, re)
            put(g, first + i + CC, im)
            grads.append((re, im))
        both = products(mo_ref[z], grads)
        for i in range(4):
            re = take(g, z * 2 * size + first + i, 8)
            im = take(g, z * 2 * size + first + i + CC, 8)
            re, im = combine(re, im, both, i, cos_own, sin_own)
            put(s, first + i, re)
            put(s, first + i + CC, im)
        return carry

    lax.fori_loop(0, CC // 4, four, 0)
    sums = [jnp.zeros((1, 128), F32)] * 2
    for half in range(2):
        rows = pl.ds(pl.multiple_of((z * 2 + swap(half)) * size, size), size)
        value = jnp.concatenate([g[0, rows, :], g[1, rows, :]], axis=1)
        g_ref[half] = value
        if second:
            sums = [sums[0] + fold(g0_ref[half] * value), sums[1] + fold(value * value)]
        else:
            sums = [sums[0] + fold(value * value), sums[1]]
        rows = pl.ds(pl.multiple_of(swap(half) * size, size), size)
        s_ref[half] = jnp.concatenate([s[0, rows, :], s[1, rows, :]], axis=1).astype(BF)
    sum_ref[...] = jnp.concatenate(sums + [jnp.zeros((6, 128), F32)], axis=0)


def window(place, blocks, constants, *more):
    return pl.pallas_call(
        lambda *refs: window_kernel(len(more) > 0, *refs),
        in_specs=[SMEM] + [VMEM] * (9 + len(more)),
        out_specs=[VMEM, VMEM, VMEM],
        out_shape=[
            jax.ShapeDtypeStruct((2, 8 * CC, 256), F32),
            jax.ShapeDtypeStruct((2, 8 * CC, 256), BF),
            jax.ShapeDtypeStruct((8, 128), F32),
        ],
        scratch_shapes=[pltpu.VMEM((2, 64 * CC, 128), F32)] * 2
        + [pltpu.VMEM((2, 16 * CC, 128), F32)],
        compiler_params=params(12),
        cost_estimate=cost(1 << 30),
        name="window",
    )(place, *blocks, *constants, *more)


def last_kernel(
    place_ref, sum_ref, i0a, i0b, i1a, i1b, data_ref, g0, g0_got, h, h_got, model_ref, res_ref
):
    core = place_ref[1]
    sums = jnp.sum(sum_ref[...], axis=1, keepdims=True)
    gg, gh, hh, ii, ij, jj = [sums[k : k + 1] for k in range(6)]
    alpha0 = gg / ii
    fresh = gg - 2.0 * alpha0 * gh + alpha0 * alpha0 * hh
    stay = 1.0 + fresh / gg
    delta = stay * stay * ii - 2.0 * stay * alpha0 * ij + alpha0 * alpha0 * jj
    alpha1 = fresh / delta
    on_first = alpha0 + alpha1 * stay
    on_second = alpha1 * alpha0
    for half in range(2):
        at = pl.ds(pl.multiple_of((half + core - 2 * half * core) * 16, 16), 16)
        for f in range(4):
            for p in range(2):
                rows = slice(f * 32 + p * 16, f * 32 + p * 16 + 16)
                left = g0[0, rows, :] if half == 0 else g0_got[rows, :]
                right = h[0, rows, :] if half == 0 else h_got[rows, :]
                model_ref[p, f, at, :] = on_first * left - on_second * right
                rows = slice(half * 32 + p * 16, half * 32 + p * 16 + 16)
                i0, i1 = ((i0a, i1a), (i0b, i1b))[f // 2]
                change = on_first * i0[f % 2, rows, :] - on_second * i1[f % 2, rows, :]
                res_ref[p, f, at, :] = data_ref[p, f, at, :] - change


def last(place, *arrays):
    shape = jax.ShapeDtypeStruct((2, 4, 32, 256), F32)
    return pl.pallas_call(
        last_kernel,
        in_specs=[SMEM] + [VMEM] * len(arrays),
        out_specs=[VMEM, VMEM],
        out_shape=[shape, shape],
        compiler_params=params(8),
        cost_estimate=cost(1 << 20),
        name="last",
    )(place, *arrays)


def total(values):
    values = values + move(values, other_core)
    for axis in (along_z, along_small, along_big):
        values = values + move(values, axis(2)) + move(values, axis(1)) + move(values, axis(3))
    return values


def body(kernel, data, cutoffs):
    rcv = lax.axis_index("rcv")
    freq = lax.axis_index("freq")
    yy, xx, zz, core = rcv // 4, rcv % 4, freq // 2, freq % 2
    place = jnp.stack([zz, core]).astype(jnp.int32)
    far = jnp.arange(16, dtype=jnp.int32) // 4
    near = jnp.arange(16, dtype=jnp.int32) % 4
    near = near % 2 * 2 + near // 2
    off_y = jnp.where(core == 0, far, near)
    off_x = jnp.where(core == 0, near, far)
    table = (yy + off_y) % 4 * 4 + (xx + off_x) % 4

    matrix = window_matrix()
    high = matrix.astype(jnp.bfloat16)
    low = (matrix - high.astype(np.float32)).astype(jnp.bfloat16)
    stacked = jnp.asarray(np.concatenate([high, low, high], axis=1))
    own_rows = stacked.reshape(2, 4, 8, 192).swapaxes(0, 1).reshape(4, 16, 192)
    bins = jnp.arange(1, F + 1, dtype=jnp.int32)
    phase = (bins[:, None] * cutoffs[None, :] % NT).astype(F32) * (2.0 * math.pi / NT)
    share = (cutoffs.astype(F32) / NT)[None, :]
    constants = (stacked, own_rows, jnp.cos(phase), jnp.sin(phase), share)

    def summed(parts):
        out = parts[0].astype(F32)
        for part in parts[1:]:
            out = out + part.astype(F32)
        return out.astype(BF)

    def sum_big(own):
        got = [move(own[kb], along_big(kb)) for kb in (2, 1, 3)]
        return [summed([own[0][ks]] + [part[ks] for part in got]) for ks in range(4)]

    def gather_terms(row):
        mine = summed([row[0]] + [move(row[n], along_small(OFFSETS[n])) for n in (1, 2, 3)])
        mine = mine.reshape(4, 2, 32, 256)
        mine = jnp.stack([mine[:, 0], move(mine[:, 1], other_core)]).reshape(256, 256)
        return [mine] + [move(mine, along_z(-k)) for k in OFFSETS[1:]]

    def image_of(shaped, i0=(None, None), early=()):
        shaped = shaped.reshape(2, 4, 32, 256)
        shaped = jnp.stack([shaped[0], move(shaped[1], other_core)], axis=1).reshape(4, 64, 256)
        row = [shaped] + [move(shaped, along_small(-ks)) for ks in OFFSETS[1:]]
        one, two = [jnp.stack([part[k : k + 2] for part in row]) for k in (0, 2)]
        near = [move(one, along_big(-kb)) for kb in (1, 3)]
        far = move(one, along_big(-2))
        (out,) = forward((0,), table, turned[0], [one])
        two, out = lax.optimization_barrier((two, out))
        near_two = [move(two, along_big(-kb)) for kb in (1, 3)]
        far_two = move(two, along_big(-2))
        (out_two,) = forward((0,), table, turned[1], [two])
        out, sums = forward((1, 3, 2), table, turned[0], near + [far], out, True, i0[0])
        out_two, out = lax.optimization_barrier((out_two, out))
        if early:
            early = (*early, sums)
            (out_two,) = forward((1, 3), table, turned[1], near_two, out_two)
            kbs, blocks = (2,), [far_two]
        else:
            kbs, blocks = (1, 3, 2), [*near_two, far_two]
        out_two, sums_two = forward(kbs, table, turned[1], blocks, out_two, True, i0[1], early)
        return (out, out_two), (sums, sums_two)

    start = jnp.swapaxes(data, 2, 3)
    out = first_adjoint(place, table, start, kernel)
    big = [pltpu.with_memory_space_constraint(t, pltpu.VMEM) for t in out[:4]]
    held, turned, own = big[:2], big[2:], out[4:]
    g0, s0, gg = window(place, gather_terms(sum_big(own)), constants)
    i0, ii = image_of(s0)
    rows = [lax.optimization_barrier(sum_big(adjoint(table, i0[k], held[k]))) for k in range(2)]
    rows = [jnp.concatenate(pair) for pair in zip(*rows)]
    h, s1, hh = window(place, gather_terms(rows), constants, g0)
    i1, sums = image_of(s1, i0, (gg, hh, *ii))
    g0_got = move(g0[1], other_core)
    h_got = move(h[1], other_core)
    model, residual = last(
        place, total(sums[1]), *i0, *i1, start, g0, g0_got, h, h_got
    )
    return jnp.swapaxes(model, 2, 3), jnp.swapaxes(residual, 2, 3)


def solution(mesh):
    placed = P(None, "freq", "rcv", None)
    return jax.shard_map(
        body,
        mesh=mesh,
        in_specs=(placed, placed, P("rcv")),
        out_specs=(placed, placed),
        check_vma=False,
    )
```
